256 devices in a mesh: dp: 8 (over x, y_lo), hid: 32 (over y_hi, z, core).
Axes of the slice: x: 4, y: 4 (y_hi: 2, y_lo: 2; y = y_hi * 2 + y_lo), z: 8, core: 2. Of those that a mesh axis runs over, the one named last changes fastest.
Arguments:
- tokens: bfloat16 [4096, 8192], P('dp', 'hid'), may hold values from -6 to 6
- cotangent: bfloat16 [4096, 8192], P('dp', 'hid'), may hold values from -6 to 6
- right_up: bfloat16 [32, 256, 1024], P('hid'), may hold values from -0.375 to 0.375
- left_up: bfloat16 [32, 1024, 1024], P('hid'), may hold values from -0.1875 to 0.1875
- left_down: bfloat16 [32, 1024, 1024], P('hid'), may hold values from -0.1875 to 0.1875
- right_down: bfloat16 [32, 1024, 256], P('hid'), may hold values from -0.1875 to 0.1875
Outputs:
- layer_out: bfloat16 [4096, 8192], P('dp', 'hid')
- tokens_grad: bfloat16 [4096, 8192], P('dp', 'hid')
- right_up_grad: float32 [32, 256, 1024], P('hid', 'dp')
- left_up_grad: float32 [32, 1024, 1024], P('hid', 'dp')
- left_down_grad: float32 [32, 1024, 1024], P('hid', 'dp')
- right_down_grad: float32 [32, 1024, 256], P('hid', 'dp')
The draws below stay inside these ranges and needn't reach their ends.
All inputs are finite; a program needn't handle non-finite values.
Results may differ from the reference program's by a relative error of at most 0.017.
Values may be sent and summed in bfloat16 or wider, within the bound.
No kernel may reach another device: no remote copies, remote signals or barrier semaphores. Data moves between devices by JAX's collectives and lax.ppermute only.
A program may use at most 64 MiB of HBM per device.

```python
import jax
import jax.numpy as jnp
from jax import lax

BLOCK = 256
UNITS_DEV = 1024
TOK_DEV = 512
TOKENS = 4096
D = 8192
N_DP = 8
N_HID = 32


def steps_of(rng, shape, split, least, top_value):
    def one(position, blocks):
        heights = jax.random.uniform(jax.random.fold_in(jax.random.fold_in(rng, 6), position), (blocks,), jnp.float32, least / len(split), top_value / len(split))
        return jnp.repeat(jnp.exp(heights), shape[position] // blocks).reshape((-1,) + (1,) * (len(shape) - position - 1))

    gain = one(*split[0])
    for cut in split[1:]:
        gain = gain * one(*cut)
    return gain


def noise(rng, shape, deviation, limit, split=(), dtype=jnp.bfloat16):
    array = jax.random.normal(rng, shape, jnp.float32) * deviation
    if len(split) > 0:
        array = steps_of(rng, shape, split, -0.22, 0.18) * array
    return jnp.clip(array, min=-limit, max=limit).astype(dtype)


def setup_inputs(seed: int = 0) -> dict:
    seeds = jax.random.split(jax.random.key(seed), 7)
    return {
        "tokens": noise(seeds[0], (TOKENS, D), 1.0, 6.0, ((0, 8), (1, 32))),
        "cotangent": noise(seeds[1], (TOKENS, D), 1.0, 6.0, ((0, 8), (1, 32))),
        "right_up": noise(seeds[2], (N_HID, BLOCK, UNITS_DEV), BLOCK ** -0.5, 0.375, ((0, 32),)),
        "left_up": noise(seeds[3], (N_HID, UNITS_DEV, UNITS_DEV), UNITS_DEV ** -0.5, 0.1875, ((0, 32),)),
        "left_down": noise(seeds[4], (N_HID, UNITS_DEV, UNITS_DEV), UNITS_DEV ** -0.5, 0.1875, ((0, 32),)),
        "right_down": noise(seeds[5], (N_HID, UNITS_DEV, BLOCK), UNITS_DEV ** -0.5, 0.1875, ((0, 32),)),
    }


def transposed(tile):
    count_tok = tile.shape[0]
    pieces = UNITS_DEV // N_HID
    return tile.reshape(count_tok, N_HID, N_HID, pieces).transpose(0, 2, 1, 3).reshape(count_tok, N_HID, UNITS_DEV)


def one_group(weights, inputs):
    right_up, left_up, left_down, right_down = weights
    x_block, c_block = inputs
    wide = jnp.float32
    grad_scale = TOKENS ** -0.5
    act_up = jnp.einsum("thb,hbk->thk", x_block.astype(wide), right_up.astype(wide)).astype(jnp.bfloat16)
    mixed_up = transposed(act_up)
    pre = jnp.einsum("tgi,gij->tgj", mixed_up.astype(wide), left_up.astype(wide))
    sigma = jax.nn.sigmoid(pre)
    hidden = (pre * sigma).astype(jnp.bfloat16)
    act_down = jnp.einsum("tgi,gij->tgj", hidden.astype(wide), left_down.astype(wide)).astype(jnp.bfloat16)
    mixed_down = transposed(act_down)
    layer_out = jnp.einsum("thk,hkb->thb", mixed_down.astype(wide), right_down.astype(wide)).astype(jnp.bfloat16)
    grad_mixed_down = jnp.einsum("thb,hkb->thk", c_block.astype(wide), right_down.astype(wide)).astype(jnp.bfloat16)
    grad_act_down = transposed(grad_mixed_down)
    grad_hidden = jnp.einsum("tgj,gij->tgi", grad_act_down.astype(wide), left_down.astype(wide))
    grad_pre = (grad_hidden * sigma * (1.0 + pre * (1.0 - sigma))).astype(jnp.bfloat16)
    grad_mixed_up = jnp.einsum("tgj,gij->tgi", grad_pre.astype(wide), left_up.astype(wide)).astype(jnp.bfloat16)
    grad_act_up = transposed(grad_mixed_up)
    tokens_grad = jnp.einsum("thk,hbk->thb", grad_act_up.astype(wide), right_up.astype(wide)).astype(jnp.bfloat16)
    part_right_up = (jnp.einsum("thb,thk->hbk", x_block.astype(wide), grad_act_up.astype(wide)) * grad_scale).astype(jnp.bfloat16)
    part_left_up = (jnp.einsum("tgi,tgj->gij", mixed_up.astype(wide), grad_pre.astype(wide)) * grad_scale).astype(jnp.bfloat16)
    part_left_down = (jnp.einsum("tgi,tgj->gij", hidden.astype(wide), grad_act_down.astype(wide)) * grad_scale).astype(jnp.bfloat16)
    part_right_down = (jnp.einsum("thk,thb->hkb", mixed_down.astype(wide), c_block.astype(wide)) * grad_scale).astype(jnp.bfloat16)
    return layer_out, tokens_grad, (part_right_up, part_left_up, part_left_down, part_right_down)


def reference(tokens, cotangent, right_up, left_up, left_down, right_down):
    x_groups = tokens.reshape(N_DP, TOK_DEV, N_HID, BLOCK)
    c_groups = cotangent.reshape(N_DP, TOK_DEV, N_HID, BLOCK)
    weights = (right_up, left_up, left_down, right_down)

    def advance(totals, inputs):
        layer_out, tokens_grad, partials = one_group(weights, inputs)
        totals = tuple(total + part.astype(jnp.float32) for total, part in zip(totals, partials))
        return totals, (layer_out, tokens_grad)

    start = tuple(jnp.zeros(weight.shape, jnp.float32) for weight in weights)
    totals, stacked = lax.scan(advance, start, (x_groups, c_groups))
    layer_out = stacked[0].reshape(TOKENS, N_HID * BLOCK)
    tokens_grad = stacked[1].reshape(TOKENS, N_HID * BLOCK)
    return layer_out, tokens_grad, totals[0], totals[1], totals[2], totals[3]
```

```python
import jax
import jax.numpy as jnp
from jax import lax
from jax.sharding import PartitionSpec as P


def contract(left_side, left_dim, right_side, right_dim):
    return lax.dot_general(
        left_side,
        right_side,
        (((left_dim,), (right_dim,)), ((), ())),
        preferred_element_type=jnp.float32,
    )


def exchange(tile):
    return lax.all_to_all(tile, "hid", 0, 0, tiled=True)


def summed(term, scale):
    part = (term * scale).astype(jnp.bfloat16)
    rows = part.shape[0] // lax.axis_size("dp")
    parts = lax.all_to_all(part, "dp", 0, 0, tiled=True).reshape(-1, rows, part.shape[1])
    return jnp.sum(parts.astype(jnp.float32), axis=0)


def body(tokens, cotangent, right_up, left_up, left_down, right_down):
    weight_ru = right_up[0]
    weight_lu = left_up[0]
    weight_ld = left_down[0]
    weight_rd = right_down[0]
    half = jnp.bfloat16
    scale = (tokens.shape[0] * lax.axis_size("dp")) ** (-0.5)
    act_up = contract(weight_ru, 0, tokens, 1).astype(half)
    mixed_up = exchange(act_up)
    grad_mixed_down = contract(weight_rd, 1, cotangent, 1).astype(half)
    grad_act_down = exchange(grad_mixed_down)
    pre = contract(weight_lu, 0, mixed_up, 0)
    sigma = jax.nn.sigmoid(pre)
    hidden = (pre * sigma).astype(half)
    act_down = contract(weight_ld, 0, hidden, 0).astype(half)
    mixed_down = exchange(act_down)
    grad_hidden = contract(weight_ld, 1, grad_act_down, 0)
    grad_pre = (grad_hidden * sigma * (1.0 + pre * (1.0 - sigma))).astype(half)
    grad_mixed_up = contract(weight_lu, 1, grad_pre, 0).astype(half)
    grad_act_up = exchange(grad_mixed_up)
    left_down_grad = summed(contract(hidden, 1, grad_act_down, 1), scale)
    left_up_grad = summed(contract(mixed_up, 1, grad_pre, 1), scale)
    layer_out = contract(mixed_down, 0, weight_rd, 0).astype(half)
    right_down_grad = summed(contract(mixed_down, 1, cotangent, 0), scale)
    tokens_grad = contract(grad_act_up, 0, weight_ru, 1).astype(half)
    right_up_grad = summed(contract(tokens, 0, grad_act_up, 1), scale)
    return (
        layer_out,
        tokens_grad,
        right_up_grad[None],
        left_up_grad[None],
        left_down_grad[None],
        right_down_grad[None],
    )


def solution(mesh):
    placed = (
        P("dp", "hid"),
        P("dp", "hid"),
        P("hid", None, None),
        P("hid", None, None),
        P("hid", None, None),
        P("hid", None, None),
    )
    return jax.shard_map(
        body,
        mesh=mesh,
        in_specs=placed,
        out_specs=(
            P("dp", "hid"),
            P("dp", "hid"),
            P("hid", "dp", None),
            P("hid", "dp", None),
            P("hid", "dp", None),
            P("hid", "dp", None),
        ),
        check_vma=False,
    )
```

```python
import jax
import jax.numpy as jnp
from jax import lax
from jax.sharding import PartitionSpec as P


def contract(left_side, left_dim, right_side, right_dim):
    return lax.dot_general(
        left_side,
        right_side,
        (((left_dim,), (right_dim,)), ((), ())),
        preferred_element_type=jnp.float32,
    )


def exchange(tile):
    return lax.all_to_all(tile, "hid", 0, 0, tiled=True)


def summed(part):
    rows = part.shape[0] // lax.axis_size("dp")
    parts = lax.all_to_all(part, "dp", 0, 0, tiled=True).reshape(-1, rows, part.shape[1])
    return jnp.sum(parts.astype(jnp.float32), axis=0)


def over_pairs(cur, axis):
    side = jnp.bitwise_and(lax.axis_index("dp"), 1)
    kept = lax.dynamic_index_in_dim(cur, side, axis, keepdims=False)
    sent = lax.dynamic_index_in_dim(cur, 1 - side, axis, keepdims=False)
    pairs = [(i, i ^ 1) for i in range(lax.axis_size("dp"))]
    got = lax.ppermute(sent, "dp", pairs)
    return kept.astype(jnp.float32) + got.astype(jnp.float32)


def over_columns(cur):
    size = lax.axis_size("dp")
    columns = size // 2
    column = jnp.right_shift(lax.axis_index("dp"), 1)
    total = None
    for step in (1, columns - 1, *range(2, columns - 1), 0):
        place = jnp.bitwise_and(column + step, columns - 1)
        block = lax.dynamic_index_in_dim(cur, place, 0, keepdims=False)
        if step:
            block = lax.ppermute(block, "dp", [(i, (i + 2 * step) % size) for i in range(size)])
        block = block.astype(jnp.float32)
        total = block if total is None else total + block
    return total


def columns_first(part):
    size = lax.axis_size("dp")
    cur = part.reshape(size // 2, 2, -1, part.shape[1])
    return over_pairs(over_columns(cur).astype(part.dtype), 0)


def pairs_first(part):
    size = lax.axis_size("dp")
    cur = part.reshape(size // 2, 2, -1, part.shape[1])
    return over_columns(over_pairs(cur, 1).astype(part.dtype))


def body(tokens, cotangent, right_up, left_up, left_down, right_down):
    weight_ru = right_up[0]
    weight_lu = left_up[0]
    weight_ld = left_down[0]
    weight_rd = right_down[0]
    half = jnp.bfloat16
    scale = (tokens.shape[0] * lax.axis_size("dp")) ** (-0.5)
    act_up = contract(weight_ru, 0, tokens, 1).astype(half)
    mixed_up = exchange(act_up)
    grad_mixed_down = contract(weight_rd, 1, cotangent, 1).astype(half)
    received = exchange(grad_mixed_down)
    pre = contract(weight_lu, 0, mixed_up, 0)
    sigma = jax.nn.sigmoid(pre)
    hidden = (pre * sigma).astype(half)
    act_down = contract(weight_ld, 0, hidden, 0).astype(half)
    grad_act_down, act_down = lax.optimization_barrier((received, act_down))
    mixed_down = exchange(act_down)
    left_down_part = (contract(hidden, 1, grad_act_down, 1) * scale).astype(half)
    left_down_grad = columns_first(left_down_part)
    grad_hidden = contract(weight_ld, 1, grad_act_down, 0)
    grad_pre = (grad_hidden * sigma * (1.0 + pre * (1.0 - sigma))).astype(half)
    left_up_part = (contract(mixed_up, 1, grad_pre, 1) * scale).astype(half)
    left_up_grad = pairs_first(left_up_part)
    grad_mixed_up = contract(weight_lu, 1, grad_pre, 0).astype(half)
    grad_act_up = exchange(grad_mixed_up)
    layer_out = contract(mixed_down, 0, weight_rd, 0).astype(half)
    right_down_part = (contract(mixed_down, 1, cotangent, 0) * scale).astype(half)
    right_down_grad = columns_first(right_down_part)
    tokens_grad = contract(grad_act_up, 0, weight_ru, 1).astype(half)
    right_up_grad = summed((contract(tokens, 0, grad_act_up, 1) * scale).astype(half))
    return (
        layer_out,
        tokens_grad,
        right_up_grad[None],
        left_up_grad[None],
        left_down_grad[None],
        right_down_grad[None],
    )


def solution(mesh):
    placed = (
        P("dp", "hid"),
        P("dp", "hid"),
        P("hid", None, None),
        P("hid", None, None),
        P("hid", None, None),
        P("hid", None, None),
    )
    return jax.shard_map(
        body,
        mesh=mesh,
        in_specs=placed,
        out_specs=(
            P("dp", "hid"),
            P("dp", "hid"),
            P("hid", "dp", None),
            P("hid", "dp", None),
            P("hid", "dp", None),
            P("hid", "dp", None),
        ),
        check_vma=False,
    )
```

```python
import jax
import jax.numpy as jnp
from jax import lax
from jax.experimental.layout import Layout, with_layout_constraint
from jax.sharding import PartitionSpec as P


def contract(left_side, left_dim, right_side, right_dim):
    return lax.dot_general(
        left_side,
        right_side,
        (((left_dim,), (right_dim,)), ((), ())),
        preferred_element_type=jnp.float32,
    )


def row_major(value):
    return with_layout_constraint(value, Layout(tuple(range(value.ndim))))


def exchange(tile):
    return lax.all_to_all(tile, "hid", 0, 0, tiled=True)


def summed(part):
    rows = part.shape[0] // lax.axis_size("dp")
    parts = lax.all_to_all(part, "dp", 0, 0, tiled=True).reshape(-1, rows, part.shape[1])
    return jnp.sum(parts.astype(jnp.float32), axis=0)


def pair_halves(cur, axis):
    side = jnp.bitwise_and(lax.axis_index("dp"), 1)
    return [
        lax.dynamic_index_in_dim(cur, place, axis, keepdims=False) for place in (side, 1 - side)
    ]


def over_pairs(halves, after=()):
    kept, sent = halves
    pairs = [(i, i ^ 1) for i in range(lax.axis_size("dp"))]
    got = lax.ppermute(sent, "dp", pairs)
    got, *_ = lax.optimization_barrier((got, *after))
    return kept.astype(jnp.float32) + got.astype(jnp.float32)


def column_blocks(cur):
    columns = cur.shape[0]
    column = jnp.right_shift(lax.axis_index("dp"), 1)
    return [
        lax.dynamic_index_in_dim(
            cur, jnp.bitwise_and(column + step, columns - 1), 0, keepdims=False
        )
        for step in column_steps(columns)
    ]


def column_steps(columns):
    return (1, columns - 1, *range(2, columns - 1), 0)


def over_columns(blocks, after=()):
    size = lax.axis_size("dp")
    *sent, kept = blocks
    got = [
        lax.ppermute(block, "dp", [(i, (i + 2 * step) % size) for i in range(size)])
        for step, block in zip(column_steps(size // 2), sent)
    ]
    got = lax.optimization_barrier((*got, *after))[: len(sent)]
    return sum((block.astype(jnp.float32) for block in got), kept.astype(jnp.float32))


def by_place(part):
    return part.reshape(lax.axis_size("dp") // 2, 2, -1, part.shape[1])


def body(tokens, cotangent, right_up, left_up, left_down, right_down):
    weight_ru = right_up[0]
    weight_lu = left_up[0]
    weight_ld = left_down[0]
    weight_rd = right_down[0]
    half = jnp.bfloat16
    scale = (tokens.shape[0] * lax.axis_size("dp")) ** (-0.5)
    act_up = contract(weight_ru, 0, tokens, 1).astype(half)
    mixed_up = exchange(act_up)
    grad_mixed_down = row_major(contract(weight_rd, 1, cotangent, 1).astype(half))
    grad_mixed_down, mixed_up = lax.optimization_barrier((grad_mixed_down, mixed_up))
    received = exchange(grad_mixed_down)
    pre = contract(weight_lu, 0, mixed_up, 0)
    sigma = jax.nn.sigmoid(pre)
    hidden = (pre * sigma).astype(half)
    act_down = contract(weight_ld, 0, hidden, 0).astype(half)
    act_down = row_major(act_down)
    grad_act_down, _ = lax.optimization_barrier((received, act_down))
    mixed_down = exchange(act_down)
    left_down_part = (contract(hidden, 1, grad_act_down, 1) * scale).astype(half)
    grad_act_down, *blocks = lax.optimization_barrier(
        (grad_act_down, *column_blocks(by_place(left_down_part)))
    )
    grad_hidden = contract(weight_ld, 1, grad_act_down, 0)
    grad_pre = (grad_hidden * sigma * (1.0 + pre * (1.0 - sigma))).astype(half)
    left_up_part = (contract(mixed_up, 1, grad_pre, 1) * scale).astype(half)
    halves = pair_halves(by_place(left_up_part), 1)
    grad_mixed_up = contract(weight_lu, 1, grad_pre, 0).astype(half)
    grad_mixed_up = row_major(grad_mixed_up)
    grad_mixed_up, mixed_down, *_ = lax.optimization_barrier(
        (grad_mixed_up, mixed_down, *halves)
    )
    left_down_half = over_columns(blocks).astype(half)
    left_down_grad = over_pairs(pair_halves(left_down_half, 0))
    left_up_half = over_pairs(halves, (left_down_half, mixed_down)).astype(half)
    left_up_grad = over_columns(column_blocks(left_up_half))
    grad_act_up = exchange(grad_mixed_up)
    layer_out = contract(mixed_down, 0, weight_rd, 0).astype(half)
    later, _ = lax.optimization_barrier((mixed_down, left_up_half))
    right_down_part = row_major((contract(later, 1, cotangent, 0) * scale).astype(half))
    right_down_half = over_columns(column_blocks(by_place(right_down_part))).astype(half)
    right_down_grad = over_pairs(pair_halves(right_down_half, 0))
    tokens_grad = contract(grad_act_up, 0, weight_ru, 1).astype(half)
    right_up_grad = summed((contract(tokens, 0, grad_act_up, 1) * scale).astype(half))
    return (
        layer_out,
        tokens_grad,
        right_up_grad[None],
        left_up_grad[None],
        left_down_grad[None],
        right_down_grad[None],
    )


def solution(mesh):
    placed = (
        P("dp", "hid"),
        P("dp", "hid"),
        P("hid", None, None),
        P("hid", None, None),
        P("hid", None, None),
        P("hid", None, None),
    )
    return jax.shard_map(
        body,
        mesh=mesh,
        in_specs=placed,
        out_specs=(
            P("dp", "hid"),
            P("dp", "hid"),
            P("hid", "dp", None),
            P("hid", "dp", None),
            P("hid", "dp", None),
            P("hid", "dp", None),
        ),
        check_vma=False,
    )
```

```python
import jax
import jax.numpy as jnp
from jax import lax
from jax.experimental.layout import Layout, with_layout_constraint
from jax.sharding import PartitionSpec as P


def contract(left_side, left_dim, right_side, right_dim):
    return lax.dot_general(
        left_side,
        right_side,
        (((left_dim,), (right_dim,)), ((), ())),
        preferred_element_type=jnp.float32,
    )


def row_major(value):
    return with_layout_constraint(value, Layout(tuple(range(value.ndim))))


def exchange(tile):
    return lax.all_to_all(tile, "hid", 0, 0, tiled=True)


def summed(part):
    rows = part.shape[0] // lax.axis_size("dp")
    parts = lax.all_to_all(part, "dp", 0, 0, tiled=True).reshape(-1, rows, part.shape[1])
    return jnp.sum(parts.astype(jnp.float32), axis=0)


def pair_halves(cur, axis):
    side = jnp.bitwise_and(lax.axis_index("dp"), 1)
    return [
        lax.dynamic_index_in_dim(cur, place, axis, keepdims=False) for place in (side, 1 - side)
    ]


def over_pairs(halves, after=()):
    kept, sent = halves
    pairs = [(i, i ^ 1) for i in range(lax.axis_size("dp"))]
    got = lax.ppermute(sent, "dp", pairs)
    got, *_ = lax.optimization_barrier((got, *after))
    return kept.astype(jnp.float32) + got.astype(jnp.float32)


def column_blocks(cur):
    column = jnp.right_shift(lax.axis_index("dp"), 1)
    own, ahead, back, far = (
        lax.dynamic_index_in_dim(
            cur, jnp.bitwise_and(column + step, cur.shape[0] - 1), 0, keepdims=False
        )
        for step in (0, 1, 3, 2)
    )
    return [own, ahead, back, far[0], far[1]]


def shifted(value, step):
    size = lax.axis_size("dp")
    return lax.ppermute(value, "dp", [(i, (i + 2 * step) % size) for i in range(size)])


def added(*terms):
    return sum((term.astype(jnp.float32) for term in terms[1:]), terms[0].astype(jnp.float32))


def first_leg(blocks):
    own, ahead, back, far_ahead, far_back = blocks
    from_back, from_ahead = shifted(far_ahead, 1), shifted(far_back, -1)
    half = own.dtype
    ahead = jnp.stack([added(ahead[0], from_back).astype(half), ahead[1]])
    back = jnp.stack([back[0], added(back[1], from_ahead).astype(half)])
    return [own, ahead, back]


def second_leg(blocks, after=()):
    own, ahead, back = blocks
    got = (shifted(ahead, 1), shifted(back, -1))
    got = lax.optimization_barrier((*got, *after))[:2]
    return added(own, *got)


def by_place(part):
    return part.reshape(lax.axis_size("dp") // 2, 2, -1, part.shape[1])


def body(tokens, cotangent, right_up, left_up, left_down, right_down):
    weight_ru = right_up[0]
    weight_lu = left_up[0]
    weight_ld = left_down[0]
    weight_rd = right_down[0]
    half = jnp.bfloat16
    scale = (tokens.shape[0] * lax.axis_size("dp")) ** (-0.5)
    act_up = contract(weight_ru, 0, tokens, 1).astype(half)
    mixed_up = exchange(act_up)
    grad_mixed_down = row_major(contract(weight_rd, 1, cotangent, 1).astype(half))
    grad_mixed_down, mixed_up = lax.optimization_barrier((grad_mixed_down, mixed_up))
    received = exchange(grad_mixed_down)
    pre = contract(weight_lu, 0, mixed_up, 0)
    sigma = jax.nn.sigmoid(pre)
    hidden = (pre * sigma).astype(half)
    act_down = contract(weight_ld, 0, hidden, 0).astype(half)
    act_down = row_major(act_down)
    grad_act_down, _ = lax.optimization_barrier((received, act_down))
    mixed_down = exchange(act_down)
    left_down_part = (contract(hidden, 1, grad_act_down, 1) * scale).astype(half)
    grad_act_down, *down_blocks = lax.optimization_barrier(
        (grad_act_down, *column_blocks(by_place(left_down_part)))
    )
    down_blocks = first_leg(down_blocks)
    grad_hidden = contract(weight_ld, 1, grad_act_down, 0)
    grad_pre = (grad_hidden * sigma * (1.0 + pre * (1.0 - sigma))).astype(half)
    left_up_part = (contract(mixed_up, 1, grad_pre, 1) * scale).astype(half)
    up_blocks = first_leg(column_blocks(by_place(left_up_part)))
    grad_mixed_up = row_major(contract(weight_lu, 1, grad_pre, 0).astype(half))
    grad_mixed_up, mixed_down, *_ = lax.optimization_barrier(
        (grad_mixed_up, mixed_down, *down_blocks, *up_blocks)
    )
    grad_act_up = exchange(grad_mixed_up)
    left_down_half = second_leg(down_blocks, (mixed_down,)).astype(half)
    left_down_grad = over_pairs(pair_halves(left_down_half, 0))
    later, _ = lax.optimization_barrier((mixed_down, mixed_down))
    right_down_part = row_major((contract(later, 1, cotangent, 0) * scale).astype(half))
    right_blocks = column_blocks(by_place(right_down_part))
    layer_out = contract(mixed_down, 0, weight_rd, 0).astype(half)
    left_up_half = second_leg(up_blocks, (mixed_down,)).astype(half)
    right_up_part = (contract(tokens, 0, grad_act_up, 1) * scale).astype(half)
    left_up_grad = over_pairs(pair_halves(left_up_half, 0))
    right_up_grad = summed(right_up_part)
    right_down_half = second_leg(first_leg(right_blocks), (right_up_part,)).astype(half)
    right_down_grad = over_pairs(pair_halves(right_down_half, 0))
    tokens_grad = contract(grad_act_up, 0, weight_ru, 1).astype(half)
    return (
        layer_out,
        tokens_grad,
        right_up_grad[None],
        left_up_grad[None],
        left_down_grad[None],
        right_down_grad[None],
    )


def solution(mesh):
    placed = (
        P("dp", "hid"),
        P("dp", "hid"),
        P("hid", None, None),
        P("hid", None, None),
        P("hid", None, None),
        P("hid", None, None),
    )
    return jax.shard_map(
        body,
        mesh=mesh,
        in_specs=placed,
        out_specs=(
            P("dp", "hid"),
            P("dp", "hid"),
            P("hid", "dp", None),
            P("hid", "dp", None),
            P("hid", "dp", None),
            P("hid", "dp", None),
        ),
        check_vma=False,
    )
```

```python
import jax
import jax.numpy as jnp
from jax import lax
from jax.experimental.layout import Layout, with_layout_constraint
from jax.sharding import PartitionSpec as P


def contract(left_side, left_dim, right_side, right_dim):
    return lax.dot_general(
        left_side,
        right_side,
        (((left_dim,), (right_dim,)), ((), ())),
        preferred_element_type=jnp.float32,
    )


def row_major(value):
    return with_layout_constraint(value, Layout(tuple(range(value.ndim))))


def exchange(tile):
    return lax.all_to_all(tile, "hid", 0, 0, tiled=True)


def summed(part):
    rows = part.shape[0] // lax.axis_size("dp")
    parts = lax.all_to_all(part, "dp", 0, 0, tiled=True).reshape(-1, rows, part.shape[1])
    return jnp.sum(parts.astype(jnp.float32), axis=0)


def pair_halves(cur, axis):
    side = jnp.bitwise_and(lax.axis_index("dp"), 1)
    return [
        lax.dynamic_index_in_dim(cur, place, axis, keepdims=False) for place in (side, 1 - side)
    ]


def over_pairs(halves, after=()):
    kept, sent = halves
    pairs = [(i, i ^ 1) for i in range(lax.axis_size("dp"))]
    got = lax.ppermute(sent, "dp", pairs)
    got, *_ = lax.optimization_barrier((got, *after))
    return kept.astype(jnp.float32) + got.astype(jnp.float32)


def column_blocks(cur):
    column = jnp.right_shift(lax.axis_index("dp"), 1)
    own, ahead, back, far = (
        lax.dynamic_index_in_dim(
            cur, jnp.bitwise_and(column + step, cur.shape[0] - 1), 0, keepdims=False
        )
        for step in (0, 1, 3, 2)
    )
    return [own, ahead, back, far[0], far[1]]


def shifted(value, step):
    size = lax.axis_size("dp")
    return lax.ppermute(value, "dp", [(i, (i + 2 * step) % size) for i in range(size)])


def added(*terms):
    return sum((term.astype(jnp.float32) for term in terms[1:]), terms[0].astype(jnp.float32))


def first_leg(blocks):
    own, ahead, back, far_ahead, far_back = blocks
    from_back, from_ahead = shifted(far_ahead, 1), shifted(far_back, -1)
    half = own.dtype
    ahead = ahead.at[0].set(added(ahead[0], from_back).astype(half))
    back = back.at[1].set(added(back[1], from_ahead).astype(half))
    return [own, ahead, back]


def second_leg(blocks, after=()):
    own, ahead, back = blocks
    got = (shifted(ahead, 1), shifted(back, -1))
    got = lax.optimization_barrier((*got, *after))[:2]
    return added(own, *got)


def by_place(part):
    return part.reshape(lax.axis_size("dp") // 2, 2, -1, part.shape[1])


def body(tokens, cotangent, right_up, left_up, left_down, right_down):
    weight_ru = right_up[0]
    weight_lu = left_up[0]
    weight_ld = left_down[0]
    weight_rd = right_down[0]
    half = jnp.bfloat16
    scale = (tokens.shape[0] * lax.axis_size("dp")) ** (-0.5)
    act_up = contract(weight_ru, 0, tokens, 1).astype(half)
    mixed_up = exchange(act_up)
    grad_mixed_down = row_major(contract(weight_rd, 1, cotangent, 1).astype(half))
    grad_mixed_down, mixed_up = lax.optimization_barrier((grad_mixed_down, mixed_up))
    received = exchange(grad_mixed_down)
    pre = contract(weight_lu, 0, mixed_up, 0)
    sigma = jax.nn.sigmoid(pre)
    hidden = (pre * sigma).astype(half)
    act_down = contract(weight_ld, 0, hidden, 0).astype(half)
    act_down = row_major(act_down)
    slope = sigma * (1.0 + pre * (1.0 - sigma))
    tokens_turned = row_major(tokens.T)
    grad_act_down, hidden, slope, tokens_turned, _ = lax.optimization_barrier(
        (received, hidden, slope, tokens_turned, act_down)
    )
    mixed_down = exchange(act_down)
    left_down_part = (contract(hidden, 1, grad_act_down, 1) * scale).astype(half)
    grad_act_down, *down_blocks = lax.optimization_barrier(
        (grad_act_down, *column_blocks(by_place(left_down_part)))
    )
    down_blocks = first_leg(down_blocks)
    grad_hidden = contract(weight_ld, 1, grad_act_down, 0)
    grad_pre = (grad_hidden * slope).astype(half)
    left_up_part = (contract(mixed_up, 1, grad_pre, 1) * scale).astype(half)
    up_blocks = first_leg(column_blocks(by_place(left_up_part)))
    grad_mixed_up = row_major(contract(weight_lu, 1, grad_pre, 0).astype(half))
    grad_mixed_up, mixed_down, *_ = lax.optimization_barrier(
        (grad_mixed_up, mixed_down, *down_blocks, *up_blocks)
    )
    grad_act_up = exchange(grad_mixed_up)
    left_down_half = second_leg(down_blocks, (mixed_down,)).astype(half)
    left_down_grad = over_pairs(pair_halves(left_down_half, 0))
    right_down_part = row_major((contract(mixed_down, 1, cotangent, 0) * scale).astype(half))
    right_blocks = column_blocks(by_place(right_down_part))
    layer_out = contract(mixed_down, 0, weight_rd, 0).astype(half)
    left_up_half = second_leg(up_blocks, (mixed_down,)).astype(half)
    right_up_part = row_major((contract(tokens_turned, 1, grad_act_up, 1) * scale).astype(half))
    left_up_grad = over_pairs(pair_halves(left_up_half, 0))
    right_up_grad = summed(right_up_part)
    right_down_half = second_leg(first_leg(right_blocks), (right_up_part,)).astype(half)
    right_down_grad = over_pairs(pair_halves(right_down_half, 0))
    tokens_grad = contract(grad_act_up, 0, weight_ru, 1).astype(half)
    return (
        layer_out,
        tokens_grad,
        right_up_grad[None],
        left_up_grad[None],
        left_down_grad[None],
        right_down_grad[None],
    )


def solution(mesh):
    placed = (
        P("dp", "hid"),
        P("dp", "hid"),
        P("hid", None, None),
        P("hid", None, None),
        P("hid", None, None),
        P("hid", None, None),
    )
    return jax.shard_map(
        body,
        mesh=mesh,
        in_specs=placed,
        out_specs=(
            P("dp", "hid"),
            P("dp", "hid"),
            P("hid", "dp", None),
            P("hid", "dp", None),
            P("hid", "dp", None),
            P("hid", "dp", None),
        ),
        check_vma=False,
    )
```

```python
import jax
import jax.numpy as jnp
from jax import lax
from jax.experimental.layout import Layout, with_layout_constraint
from jax.sharding import PartitionSpec as P


def contract(left_side, left_dim, right_side, right_dim):
    return lax.dot_general(
        left_side,
        right_side,
        (((left_dim,), (right_dim,)), ((), ())),
        preferred_element_type=jnp.float32,
    )


def row_major(value):
    return with_layout_constraint(value, Layout(tuple(range(value.ndim))))


def exchange(tile):
    return lax.all_to_all(tile, "hid", 0, 0, tiled=True)


def summed(part):
    rows = part.shape[0] // lax.axis_size("dp")
    parts = lax.all_to_all(part, "dp", 0, 0, tiled=True).reshape(-1, rows, part.shape[1])
    return jnp.sum(parts.astype(jnp.float32), axis=0)


def pair_halves(cur, axis):
    side = jnp.bitwise_and(lax.axis_index("dp"), 1)
    return [
        lax.dynamic_index_in_dim(cur, place, axis, keepdims=False) for place in (side, 1 - side)
    ]


def over_pairs(halves, after=()):
    kept, sent = halves
    pairs = [(i, i ^ 1) for i in range(lax.axis_size("dp"))]
    got = lax.ppermute(sent, "dp", pairs)
    got, *_ = lax.optimization_barrier((got, *after))
    return kept.astype(jnp.float32) + got.astype(jnp.float32)


def column_blocks(cur):
    column = jnp.right_shift(lax.axis_index("dp"), 1)
    own, ahead, back, far = (
        lax.dynamic_index_in_dim(
            cur, jnp.bitwise_and(column + step, cur.shape[0] - 1), 0, keepdims=False
        )
        for step in (0, 1, 3, 2)
    )
    return [own, ahead, back, far[0], far[1]]


def shifted(value, step):
    size = lax.axis_size("dp")
    return lax.ppermute(value, "dp", [(i, (i + 2 * step) % size) for i in range(size)])


def added(*terms):
    return sum((term.astype(jnp.float32) for term in terms[1:]), terms[0].astype(jnp.float32))


def first_leg(blocks):
    own, ahead, back, far_ahead, far_back = blocks
    from_back, from_ahead = shifted(far_ahead, 1), shifted(far_back, -1)
    half = own.dtype
    ahead = ahead.at[0].set(added(ahead[0], from_back).astype(half))
    back = back.at[1].set(added(back[1], from_ahead).astype(half))
    return [own, ahead, back]


def second_leg(blocks, after=()):
    own, ahead, back = blocks
    got = (shifted(ahead, 1), shifted(back, -1))
    got = lax.optimization_barrier((*got, *after))[:2]
    return added(own, *got)


def by_place(part):
    return part.reshape(lax.axis_size("dp") // 2, 2, -1, part.shape[1])


def body(tokens, cotangent, right_up, left_up, left_down, right_down):
    weight_ru = right_up[0]
    weight_lu = left_up[0]
    weight_ld = left_down[0]
    weight_rd = right_down[0]
    half = jnp.bfloat16
    scale = (tokens.shape[0] * lax.axis_size("dp")) ** (-0.5)
    act_up = contract(weight_ru, 0, tokens, 1).astype(half)
    mixed_up = exchange(act_up)
    grad_mixed_down = row_major(contract(weight_rd, 1, cotangent, 1).astype(half))
    grad_mixed_down, mixed_up = lax.optimization_barrier((grad_mixed_down, mixed_up))
    received = exchange(grad_mixed_down)
    pre = contract(weight_lu, 0, mixed_up, 0)
    sigma = jax.nn.sigmoid(pre)
    hidden = (pre * sigma).astype(half)
    act_down = contract(weight_ld, 0, hidden, 0).astype(half)
    act_down = row_major(act_down)
    slope = sigma * (1.0 + pre * (1.0 - sigma))
    tokens_turned = row_major(tokens.T)
    grad_act_down, hidden, slope, tokens_turned, _ = lax.optimization_barrier(
        (received, hidden, slope, tokens_turned, act_down)
    )
    mixed_down = exchange(act_down)
    left_down_part = (contract(hidden, 1, grad_act_down, 1) * scale).astype(half)
    left_down_sum = lax.psum_scatter(left_down_part, "dp", scatter_dimension=0, tiled=True)
    grad_act_down, _ = lax.optimization_barrier((grad_act_down, left_down_part))
    grad_hidden = contract(weight_ld, 1, grad_act_down, 0)
    grad_pre = (grad_hidden * slope).astype(half)
    left_up_part = (contract(mixed_up, 1, grad_pre, 1) * scale).astype(half)
    up_blocks = first_leg(column_blocks(by_place(left_up_part)))
    grad_mixed_up = row_major(contract(weight_lu, 1, grad_pre, 0).astype(half))
    grad_mixed_up, mixed_down, *_ = lax.optimization_barrier(
        (grad_mixed_up, mixed_down, *up_blocks)
    )
    grad_act_up = exchange(grad_mixed_up)
    right_down_part = row_major((contract(mixed_down, 1, cotangent, 0) * scale).astype(half))
    right_blocks = column_blocks(by_place(right_down_part))
    layer_out = contract(mixed_down, 0, weight_rd, 0).astype(half)
    left_up_half = second_leg(up_blocks, (mixed_down,)).astype(half)
    right_up_part = row_major((contract(tokens_turned, 1, grad_act_up, 1) * scale).astype(half))
    left_up_grad = over_pairs(pair_halves(left_up_half, 0))
    right_up_grad = summed(right_up_part)
    right_down_half = second_leg(first_leg(right_blocks), (right_up_part,)).astype(half)
    right_down_grad = over_pairs(pair_halves(right_down_half, 0))
    tokens_grad = contract(grad_act_up, 0, weight_ru, 1).astype(half)
    return (
        layer_out,
        tokens_grad,
        right_up_grad[None],
        left_up_grad[None],
        left_down_sum.astype(jnp.float32)[None],
        right_down_grad[None],
    )


def solution(mesh):
    placed = (
        P("dp", "hid"),
        P("dp", "hid"),
        P("hid", None, None),
        P("hid", None, None),
        P("hid", None, None),
        P("hid", None, None),
    )
    return jax.shard_map(
        body,
        mesh=mesh,
        in_specs=placed,
        out_specs=(
            P("dp", "hid"),
            P("dp", "hid"),
            P("hid", "dp", None),
            P("hid", "dp", None),
            P("hid", "dp", None),
            P("hid", "dp", None),
        ),
        check_vma=False,
    )
```

```python
import jax
import jax.numpy as jnp
from jax import lax
from jax.experimental.layout import Layout, with_layout_constraint
from jax.sharding import PartitionSpec as P


def contract(left_side, left_dim, right_side, right_dim):
    return lax.dot_general(
        left_side,
        right_side,
        (((left_dim,), (right_dim,)), ((), ())),
        preferred_element_type=jnp.float32,
    )


def row_major(value):
    return with_layout_constraint(value, Layout(tuple(range(value.ndim))))


def exchange(tile):
    return lax.all_to_all(tile, "hid", 0, 0, tiled=True)


def summed(part):
    rows = part.shape[0] // lax.axis_size("dp")
    parts = lax.all_to_all(part, "dp", 0, 0, tiled=True).reshape(-1, rows, part.shape[1])
    return jnp.sum(parts.astype(jnp.float32), axis=0)


def pair_halves(cur, axis):
    side = jnp.bitwise_and(lax.axis_index("dp"), 1)
    return [
        lax.dynamic_index_in_dim(cur, place, axis, keepdims=False) for place in (side, 1 - side)
    ]


def over_pairs(halves, after=()):
    kept, sent = halves
    pairs = [(i, i ^ 1) for i in range(lax.axis_size("dp"))]
    got = lax.ppermute(sent, "dp", pairs)
    got, *_ = lax.optimization_barrier((got, *after))
    return kept.astype(jnp.float32) + got.astype(jnp.float32)


def column_blocks(cur):
    column = jnp.right_shift(lax.axis_index("dp"), 1)
    own, ahead, back, far = (
        lax.dynamic_index_in_dim(
            cur, jnp.bitwise_and(column + step, cur.shape[0] - 1), 0, keepdims=False
        )
        for step in (0, 1, 3, 2)
    )
    return [own, ahead, back, far[0], far[1]]


def shifted(value, step):
    size = lax.axis_size("dp")
    return lax.ppermute(value, "dp", [(i, (i + 2 * step) % size) for i in range(size)])


def added(*terms):
    return sum((term.astype(jnp.float32) for term in terms[1:]), terms[0].astype(jnp.float32))


def first_leg(blocks, after=()):
    own, ahead, back, far_ahead, far_back = blocks
    got = (shifted(far_ahead, 1), shifted(far_back, -1))
    from_back, from_ahead = lax.optimization_barrier((*got, *after))[:2]
    half = own.dtype
    ahead = ahead.at[0].set(added(ahead[0], from_back).astype(half))
    back = back.at[1].set(added(back[1], from_ahead).astype(half))
    return [own, ahead, back]


def second_leg(blocks, after=()):
    own, ahead, back = blocks
    got = (shifted(ahead, 1), shifted(back, -1))
    got = lax.optimization_barrier((*got, *after))[:2]
    return added(own, *got)


def by_place(part):
    return part.reshape(lax.axis_size("dp") // 2, 2, -1, part.shape[1])


def body(tokens, cotangent, right_up, left_up, left_down, right_down):
    weight_ru = right_up[0]
    weight_lu = left_up[0]
    weight_ld = left_down[0]
    weight_rd = right_down[0]
    half = jnp.bfloat16
    scale = (tokens.shape[0] * lax.axis_size("dp")) ** (-0.5)
    act_up = contract(weight_ru, 0, tokens, 1).astype(half)
    mixed_up = exchange(act_up)
    grad_mixed_down = row_major(contract(weight_rd, 1, cotangent, 1).astype(half))
    grad_mixed_down, mixed_up = lax.optimization_barrier((grad_mixed_down, mixed_up))
    received = exchange(grad_mixed_down)
    pre = contract(weight_lu, 0, mixed_up, 0)
    sigma = jax.nn.sigmoid(pre)
    hidden = (pre * sigma).astype(half)
    act_down = contract(weight_ld, 0, hidden, 0).astype(half)
    act_down = row_major(act_down)
    slope = sigma * (1.0 + pre * (1.0 - sigma))
    tokens_turned = row_major(tokens.T)
    grad_act_down, hidden, slope, tokens_turned, _ = lax.optimization_barrier(
        (received, hidden, slope, tokens_turned, act_down)
    )
    mixed_down = exchange(act_down)
    left_down_part = (contract(hidden, 1, grad_act_down, 1) * scale).astype(half)
    grad_act_down, *down_blocks = lax.optimization_barrier(
        (grad_act_down, *column_blocks(by_place(left_down_part)))
    )
    down_blocks = first_leg(down_blocks)
    grad_hidden = contract(weight_ld, 1, grad_act_down, 0)
    grad_pre = (grad_hidden * slope).astype(half)
    left_up_part = (contract(mixed_up, 1, grad_pre, 1) * scale).astype(half)
    up_blocks = column_blocks(by_place(left_up_part))
    grad_mixed_up = row_major(contract(weight_lu, 1, grad_pre, 0).astype(half))
    grad_mixed_up, mixed_down, *_ = lax.optimization_barrier(
        (grad_mixed_up, mixed_down, *down_blocks, *up_blocks)
    )
    grad_act_up = exchange(grad_mixed_up)
    left_down_half = second_leg(down_blocks, (mixed_down,)).astype(half)
    down_halves = pair_halves(left_down_half, 0)
    right_down_part = row_major((contract(mixed_down, 1, cotangent, 0) * scale).astype(half))
    right_blocks = column_blocks(by_place(right_down_part))
    layer_out = contract(mixed_down, 0, weight_rd, 0).astype(half)
    left_up_half = second_leg(first_leg(up_blocks, (mixed_down,)), down_halves).astype(half)
    right_up_part = row_major((contract(tokens_turned, 1, grad_act_up, 1) * scale).astype(half))
    up_halves = pair_halves(left_up_half, 0)
    left_down_grad = over_pairs(down_halves, up_halves)
    left_up_grad = over_pairs(up_halves, (right_up_part,))
    right_up_grad = summed(right_up_part)
    right_down_half = second_leg(first_leg(right_blocks), (right_up_part,)).astype(half)
    right_down_grad = over_pairs(pair_halves(right_down_half, 0))
    grad_act_up, _ = lax.optimization_barrier((grad_act_up, left_up_grad))
    tokens_grad = contract(grad_act_up, 0, weight_ru, 1).astype(half)
    return (
        layer_out,
        tokens_grad,
        right_up_grad[None],
        left_up_grad[None],
        left_down_grad[None],
        right_down_grad[None],
    )


def solution(mesh):
    placed = (
        P("dp", "hid"),
        P("dp", "hid"),
        P("hid", None, None),
        P("hid", None, None),
        P("hid", None, None),
        P("hid", None, None),
    )
    return jax.shard_map(
        body,
        mesh=mesh,
        in_specs=placed,
        out_specs=(
            P("dp", "hid"),
            P("dp", "hid"),
            P("hid", "dp", None),
            P("hid", "dp", None),
            P("hid", "dp", None),
            P("hid", "dp", None),
        ),
        check_vma=False,
    )
```

```python
import jax
import jax.numpy as jnp
from jax import lax
from jax.experimental.layout import Layout, with_layout_constraint
from jax.sharding import PartitionSpec as P


def contract(left_side, left_dim, right_side, right_dim):
    return lax.dot_general(
        left_side,
        right_side,
        (((left_dim,), (right_dim,)), ((), ())),
        preferred_element_type=jnp.float32,
    )


def row_major(value):
    return with_layout_constraint(value, Layout(tuple(range(value.ndim))))


def exchange(tile):
    return lax.all_to_all(tile, "hid", 0, 0, tiled=True)


def summed(part):
    rows = part.shape[0] // lax.axis_size("dp")
    parts = lax.all_to_all(part, "dp", 0, 0, tiled=True).reshape(-1, rows, part.shape[1])
    return jnp.sum(parts.astype(jnp.float32), axis=0)


def pair_halves(cur, axis, bit=0):
    side = jnp.bitwise_and(jnp.right_shift(lax.axis_index("dp"), bit), 1)
    return [
        lax.dynamic_index_in_dim(cur, place, axis, keepdims=False) for place in (side, 1 - side)
    ]


def over_pairs(halves, after=(), bit=0):
    kept, sent = halves
    pairs = [(i, i ^ (1 << bit)) for i in range(lax.axis_size("dp"))]
    got = lax.ppermute(sent, "dp", pairs)
    got, *_ = lax.optimization_barrier((got, *after))
    return kept.astype(jnp.float32) + got.astype(jnp.float32)


def column_blocks(cur):
    column = jnp.right_shift(lax.axis_index("dp"), 1)
    own, ahead, back, far = (
        lax.dynamic_index_in_dim(
            cur, jnp.bitwise_and(column + step, cur.shape[0] - 1), 0, keepdims=False
        )
        for step in (0, 1, 3, 2)
    )
    return [own, ahead, back, far[0], far[1]]


def shifted(value, step):
    size = lax.axis_size("dp")
    return lax.ppermute(value, "dp", [(i, (i + 2 * step) % size) for i in range(size)])


def added(*terms):
    return sum((term.astype(jnp.float32) for term in terms[1:]), terms[0].astype(jnp.float32))


def first_leg(blocks, after=()):
    own, ahead, back, far_ahead, far_back = blocks
    got = (shifted(far_ahead, 1), shifted(far_back, -1))
    from_back, from_ahead = lax.optimization_barrier((*got, *after))[:2]
    half = own.dtype
    ahead = ahead.at[0].set(added(ahead[0], from_back).astype(half))
    back = back.at[1].set(added(back[1], from_ahead).astype(half))
    return [own, ahead, back]


def second_leg(blocks, after=()):
    own, ahead, back = blocks
    got = (shifted(ahead, 1), shifted(back, -1))
    got = lax.optimization_barrier((*got, *after))[:2]
    return added(own, *got)


def by_place(part):
    return part.reshape(lax.axis_size("dp") // 2, 2, -1, part.shape[1])


def body(tokens, cotangent, right_up, left_up, left_down, right_down):
    weight_ru = right_up[0]
    weight_lu = left_up[0]
    weight_ld = left_down[0]
    weight_rd = right_down[0]
    half = jnp.bfloat16
    scale = (tokens.shape[0] * lax.axis_size("dp")) ** (-0.5)
    act_up = contract(weight_ru, 0, tokens, 1).astype(half)
    mixed_up = exchange(act_up)
    grad_mixed_down = row_major(contract(weight_rd, 1, cotangent, 1).astype(half))
    grad_mixed_down, mixed_up = lax.optimization_barrier((grad_mixed_down, mixed_up))
    received = exchange(grad_mixed_down)
    pre = contract(weight_lu, 0, mixed_up, 0)
    sigma = jax.nn.sigmoid(pre)
    hidden = (pre * sigma).astype(half)
    act_down = contract(weight_ld, 0, hidden, 0).astype(half)
    act_down = row_major(act_down)
    slope = sigma * (1.0 + pre * (1.0 - sigma))
    tokens_turned = row_major(tokens.T)
    grad_act_down, hidden, slope, tokens_turned, _ = lax.optimization_barrier(
        (received, hidden, slope, tokens_turned, act_down)
    )
    mixed_down = exchange(act_down)
    left_down_part = (contract(hidden, 1, grad_act_down, 1) * scale).astype(half)
    grad_act_down, *down_blocks = lax.optimization_barrier(
        (grad_act_down, *column_blocks(by_place(left_down_part)))
    )
    down_blocks = first_leg(down_blocks)
    grad_hidden = contract(weight_ld, 1, grad_act_down, 0)
    grad_pre = (grad_hidden * slope).astype(half)
    left_up_part = (contract(mixed_up, 1, grad_pre, 1) * scale).astype(half)
    up_blocks = column_blocks(by_place(left_up_part))
    grad_mixed_up = row_major(contract(weight_lu, 1, grad_pre, 0).astype(half))
    grad_mixed_up, mixed_down, *_ = lax.optimization_barrier(
        (grad_mixed_up, mixed_down, *down_blocks, *up_blocks)
    )
    grad_act_up = exchange(grad_mixed_up)
    up_blocks = first_leg(up_blocks, (mixed_down,))
    later, *up_blocks = lax.optimization_barrier((mixed_down, *up_blocks))
    left_down_half = second_leg(down_blocks, (mixed_down,)).astype(half)
    down_halves = pair_halves(left_down_half, 0)
    right_down_part = row_major((contract(later, 1, cotangent, 0) * scale).astype(half))
    right_cur = right_down_part.reshape(2, 2, 2, -1, right_down_part.shape[1])
    right_halves = pair_halves(right_cur, 0, 2)
    layer_out = contract(mixed_down, 0, weight_rd, 0).astype(half)
    left_up_half = second_leg(up_blocks, down_halves).astype(half)
    right_up_part = row_major((contract(tokens_turned, 1, grad_act_up, 1) * scale).astype(half))
    up_halves = pair_halves(left_up_half, 0)
    left_down_grad = over_pairs(down_halves, up_halves)
    left_up_grad = over_pairs(up_halves, (right_up_part,))
    right_up_grad = summed(right_up_part)
    right_cur = over_pairs(right_halves, down_halves, 2).astype(half)
    right_cur = over_pairs(pair_halves(right_cur, 0, 1), (right_up_part,), 1).astype(half)
    right_down_grad = over_pairs(pair_halves(right_cur, 0), ())
    grad_act_up, _ = lax.optimization_barrier((grad_act_up, left_up_grad))
    tokens_grad = contract(grad_act_up, 0, weight_ru, 1).astype(half)
    return (
        layer_out,
        tokens_grad,
        right_up_grad[None],
        left_up_grad[None],
        left_down_grad[None],
        right_down_grad[None],
    )


def solution(mesh):
    placed = (
        P("dp", "hid"),
        P("dp", "hid"),
        P("hid", None, None),
        P("hid", None, None),
        P("hid", None, None),
        P("hid", None, None),
    )
    return jax.shard_map(
        body,
        mesh=mesh,
        in_specs=placed,
        out_specs=(
            P("dp", "hid"),
            P("dp", "hid"),
            P("hid", "dp", None),
            P("hid", "dp", None),
            P("hid", "dp", None),
            P("hid", "dp", None),
        ),
        check_vma=False,
    )
```

```python
import jax
import jax.numpy as jnp
from jax import lax
from jax.experimental.layout import Layout, with_layout_constraint
from jax.sharding import PartitionSpec as P


def contract(left_side, left_dim, right_side, right_dim):
    return lax.dot_general(
        left_side,
        right_side,
        (((left_dim,), (right_dim,)), ((), ())),
        preferred_element_type=jnp.float32,
    )


def row_major(value):
    return with_layout_constraint(value, Layout(tuple(range(value.ndim))))


def exchange(tile):
    return lax.all_to_all(tile, "hid", 0, 0, tiled=True)


def collected(part):
    rows = part.shape[0] // lax.axis_size("dp")
    return lax.all_to_all(part, "dp", 0, 0, tiled=True).reshape(-1, rows, part.shape[1])


def pair_halves(cur, axis, bit=0):
    side = jnp.bitwise_and(jnp.right_shift(lax.axis_index("dp"), bit), 1)
    return [
        lax.dynamic_index_in_dim(cur, place, axis, keepdims=False) for place in (side, 1 - side)
    ]


def paired(value, bit=0):
    return lax.ppermute(value, "dp", [(i, i ^ (1 << bit)) for i in range(lax.axis_size("dp"))])


def column_blocks(cur):
    column = jnp.right_shift(lax.axis_index("dp"), 1)
    own, ahead, back, far = (
        lax.dynamic_index_in_dim(
            cur, jnp.bitwise_and(column + step, cur.shape[0] - 1), 0, keepdims=False
        )
        for step in (0, 1, 3, 2)
    )
    return [own, ahead, back, far[0], far[1]]


def shifted(value, step):
    size = lax.axis_size("dp")
    return lax.ppermute(value, "dp", [(i, (i + 2 * step) % size) for i in range(size)])


def added(*terms):
    return sum((term.astype(jnp.float32) for term in terms[1:]), terms[0].astype(jnp.float32))


def first_leg(blocks, after=()):
    own, ahead, back, far_ahead, far_back = blocks
    got = (shifted(far_ahead, 1), shifted(far_back, -1))
    from_back, from_ahead = lax.optimization_barrier((*got, *after))[:2]
    half = own.dtype
    ahead = ahead.at[0].set(added(ahead[0], from_back).astype(half))
    back = back.at[1].set(added(back[1], from_ahead).astype(half))
    return [own, ahead, back]


def second_leg(blocks, after=()):
    own, ahead, back = blocks
    got = (shifted(ahead, 1), shifted(back, -1))
    got = lax.optimization_barrier((*got, *after))[:2]
    return added(own, *got)


def by_place(part):
    return part.reshape(lax.axis_size("dp") // 2, 2, -1, part.shape[1])


def body(tokens, cotangent, right_up, left_up, left_down, right_down):
    weight_ru = right_up[0]
    weight_lu = left_up[0]
    weight_ld = left_down[0]
    weight_rd = right_down[0]
    half = jnp.bfloat16
    scale = (tokens.shape[0] * lax.axis_size("dp")) ** (-0.5)
    act_up = contract(weight_ru, 0, tokens, 1).astype(half)
    mixed_up = exchange(act_up)
    grad_mixed_down = row_major(contract(weight_rd, 1, cotangent, 1).astype(half))
    grad_mixed_down, mixed_up = lax.optimization_barrier((grad_mixed_down, mixed_up))
    received = exchange(grad_mixed_down)
    pre = contract(weight_lu, 0, mixed_up, 0)
    sigma = jax.nn.sigmoid(pre)
    hidden = (pre * sigma).astype(half)
    act_down = contract(weight_ld, 0, hidden, 0).astype(half)
    act_down = row_major(act_down)
    slope = sigma * (1.0 + pre * (1.0 - sigma))
    tokens_turned = row_major(tokens.T)
    grad_act_down, hidden, slope, tokens_turned, _ = lax.optimization_barrier(
        (received, hidden, slope, tokens_turned, act_down)
    )
    mixed_down = exchange(act_down)
    left_down_part = (contract(hidden, 1, grad_act_down, 1) * scale).astype(half)
    grad_act_down, *down_blocks = lax.optimization_barrier(
        (grad_act_down, *column_blocks(by_place(left_down_part)))
    )
    down_blocks = first_leg(down_blocks)
    grad_hidden = contract(weight_ld, 1, grad_act_down, 0)
    grad_pre = (grad_hidden * slope).astype(half)
    left_up_part = (contract(mixed_up, 1, grad_pre, 1) * scale).astype(half)
    up_blocks = column_blocks(by_place(left_up_part))
    grad_mixed_up = row_major(contract(weight_lu, 1, grad_pre, 0).astype(half))
    grad_mixed_up, mixed_down, *_ = lax.optimization_barrier(
        (grad_mixed_up, mixed_down, *down_blocks, *up_blocks)
    )
    grad_act_up = exchange(grad_mixed_up)
    up_blocks = first_leg(up_blocks, (mixed_down,))
    later, *up_blocks = lax.optimization_barrier((mixed_down, *up_blocks))
    left_down_half = second_leg(down_blocks, (mixed_down,)).astype(half)
    down_halves = pair_halves(left_down_half, 0)
    right_down_part = row_major((contract(later, 1, cotangent, 0) * scale).astype(half))
    right_cur = right_down_part.reshape(2, 2, 2, -1, right_down_part.shape[1])
    right_halves = pair_halves(right_cur, 0, 2)
    layer_out = contract(mixed_down, 0, weight_rd, 0).astype(half)
    left_up_half = second_leg(up_blocks, down_halves).astype(half)
    right_up_part = row_major((contract(tokens_turned, 1, grad_act_up, 1) * scale).astype(half))
    up_halves = pair_halves(left_up_half, 0)
    right_kept, right_sent = right_halves
    right_got, *_ = lax.optimization_barrier((paired(right_sent, 2), *down_halves))
    right_cur = added(right_kept, right_got).astype(half)
    right_kept, right_sent = pair_halves(right_cur, 0, 1)
    right_got = paired(right_sent, 1)
    right_kept, right_sent = pair_halves(added(right_kept, right_got).astype(half), 0)
    right_got = paired(right_sent)
    down_got, up_got = paired(down_halves[1]), paired(up_halves[1])
    right_up_parts = collected(right_up_part)
    down_got, up_got, right_got, right_up_parts = lax.optimization_barrier(
        (down_got, up_got, right_got, right_up_parts)
    )
    left_down_grad = added(down_halves[0], down_got)
    left_up_grad = added(up_halves[0], up_got)
    right_up_grad = added(*right_up_parts)
    right_down_grad = added(right_kept, right_got)
    tokens_grad = contract(grad_act_up, 0, weight_ru, 1).astype(half)
    return (
        layer_out,
        tokens_grad,
        right_up_grad[None],
        left_up_grad[None],
        left_down_grad[None],
        right_down_grad[None],
    )


def solution(mesh):
    placed = (
        P("dp", "hid"),
        P("dp", "hid"),
        P("hid", None, None),
        P("hid", None, None),
        P("hid", None, None),
        P("hid", None, None),
    )
    return jax.shard_map(
        body,
        mesh=mesh,
        in_specs=placed,
        out_specs=(
            P("dp", "hid"),
            P("dp", "hid"),
            P("hid", "dp", None),
            P("hid", "dp", None),
            P("hid", "dp", None),
            P("hid", "dp", None),
        ),
        check_vma=False,
    )
```

```python
import jax
import jax.numpy as jnp
from jax import lax
from jax.experimental.layout import Layout, with_layout_constraint
from jax.experimental import pallas as pl
from jax.experimental.pallas import tpu as pltpu
from jax.sharding import PartitionSpec as P


def contract(left_side, left_dim, right_side, right_dim):
    return lax.dot_general(
        left_side,
        right_side,
        (((left_dim,), (right_dim,)), ((), ())),
        preferred_element_type=jnp.float32,
    )


def row_major(value):
    return with_layout_constraint(value, Layout(tuple(range(value.ndim))))


def exchange(tile):
    return lax.all_to_all(tile, "hid", 0, 0, tiled=True)


def collected(part):
    rows = part.shape[0] // lax.axis_size("dp")
    return lax.all_to_all(part, "dp", 0, 0, tiled=True).reshape(-1, rows, part.shape[1])


def pair_halves(cur, axis, bit=0):
    side = jnp.bitwise_and(jnp.right_shift(lax.axis_index("dp"), bit), 1)
    return [
        lax.dynamic_index_in_dim(cur, place, axis, keepdims=False) for place in (side, 1 - side)
    ]


def paired(value, bit=0):
    return lax.ppermute(value, "dp", [(i, i ^ (1 << bit)) for i in range(lax.axis_size("dp"))])


def column_blocks(cur):
    column = jnp.right_shift(lax.axis_index("dp"), 1)
    own, ahead, back, far = (
        lax.dynamic_index_in_dim(
            cur, jnp.bitwise_and(column + step, cur.shape[0] - 1), 0, keepdims=False
        )
        for step in (0, 1, 3, 2)
    )
    return [own, ahead, back, far[0], far[1]]


def shifted(value, step):
    size = lax.axis_size("dp")
    return lax.ppermute(value, "dp", [(i, (i + 2 * step) % size) for i in range(size)])


def added(*terms):
    return sum((term.astype(jnp.float32) for term in terms[1:]), terms[0].astype(jnp.float32))


def first_leg(blocks, after=()):
    own, ahead, back, far_ahead, far_back = blocks
    got = (shifted(far_ahead, 1), shifted(far_back, -1))
    from_back, from_ahead = lax.optimization_barrier((*got, *after))[:2]
    half = own.dtype
    ahead = ahead.at[0].set(added(ahead[0], from_back).astype(half))
    back = back.at[1].set(added(back[1], from_ahead).astype(half))
    return [own, ahead, back]


def second_leg(blocks, after=()):
    own, ahead, back = blocks
    got = (shifted(ahead, 1), shifted(back, -1))
    got = lax.optimization_barrier((*got, *after))[:2]
    return added(own, *got)


def by_place(part):
    return part.reshape(lax.axis_size("dp") // 2, 2, -1, part.shape[1])


def final_kernel(parts, *refs):
    wide = jnp.float32
    *pairs, parts_out, first_out, second_out, third_out = refs
    total = parts[0].astype(wide)
    for place in range(1, parts.shape[0]):
        total = total + parts[place].astype(wide)
    parts_out[...] = total
    for place, out in enumerate((first_out, second_out, third_out)):
        kept, got = pairs[2 * place], pairs[2 * place + 1]
        out[...] = kept[...].astype(wide) + got[...].astype(wide)


def final_sums(parts, *pairs):
    shapes = [parts.shape[1:]] + [kept.shape for kept, _ in pairs]
    reads = sum(value.size for pair in pairs for value in pair) + parts.size
    writes = sum(shape[0] * shape[1] for shape in shapes)
    return pl.pallas_call(
        final_kernel,
        out_shape=[jax.ShapeDtypeStruct(shape, jnp.float32) for shape in shapes],
        compiler_params=pltpu.CompilerParams(vmem_limit_bytes=16 * 1024 * 1024),
        cost_estimate=pl.CostEstimate(
            flops=reads, bytes_accessed=2 * reads + 4 * writes, transcendentals=0
        ),
    )(parts, *(value for pair in pairs for value in pair))


def body(tokens, cotangent, right_up, left_up, left_down, right_down):
    weight_ru = right_up[0]
    weight_lu = left_up[0]
    weight_ld = left_down[0]
    weight_rd = right_down[0]
    half = jnp.bfloat16
    scale = (tokens.shape[0] * lax.axis_size("dp")) ** (-0.5)
    act_up = contract(weight_ru, 0, tokens, 1).astype(half)
    mixed_up = exchange(act_up)
    grad_mixed_down = row_major(contract(weight_rd, 1, cotangent, 1).astype(half))
    grad_mixed_down, mixed_up = lax.optimization_barrier((grad_mixed_down, mixed_up))
    received = exchange(grad_mixed_down)
    pre = contract(weight_lu, 0, mixed_up, 0)
    sigma = jax.nn.sigmoid(pre)
    hidden = (pre * sigma).astype(half)
    act_down = contract(weight_ld, 0, hidden, 0).astype(half)
    act_down = row_major(act_down)
    slope = sigma * (1.0 + pre * (1.0 - sigma))
    tokens_turned = row_major(tokens.T)
    grad_act_down, hidden, slope, tokens_turned, _ = lax.optimization_barrier(
        (received, hidden, slope, tokens_turned, act_down)
    )
    mixed_down = exchange(act_down)
    left_down_part = (contract(hidden, 1, grad_act_down, 1) * scale).astype(half)
    grad_act_down, *down_blocks = lax.optimization_barrier(
        (grad_act_down, *column_blocks(by_place(left_down_part)))
    )
    down_blocks = first_leg(down_blocks)
    grad_hidden = contract(weight_ld, 1, grad_act_down, 0)
    grad_pre = (grad_hidden * slope).astype(half)
    left_up_part = (contract(mixed_up, 1, grad_pre, 1) * scale).astype(half)
    up_blocks = column_blocks(by_place(left_up_part))
    grad_mixed_up = row_major(contract(weight_lu, 1, grad_pre, 0).astype(half))
    grad_mixed_up, mixed_down, *_ = lax.optimization_barrier(
        (grad_mixed_up, mixed_down, *down_blocks, *up_blocks)
    )
    grad_act_up = exchange(grad_mixed_up)
    up_blocks = first_leg(up_blocks, (mixed_down,))
    later, *up_blocks = lax.optimization_barrier((mixed_down, *up_blocks))
    left_down_half = second_leg(down_blocks, (mixed_down,)).astype(half)
    down_halves = pair_halves(left_down_half, 0)
    right_down_part = row_major((contract(later, 1, cotangent, 0) * scale).astype(half))
    right_cur = right_down_part.reshape(2, 2, 2, -1, right_down_part.shape[1])
    right_halves = pair_halves(right_cur, 0, 2)
    layer_out = contract(mixed_down, 0, weight_rd, 0).astype(half)
    left_up_half = second_leg(up_blocks, down_halves).astype(half)
    right_up_part = row_major((contract(tokens_turned, 1, grad_act_up, 1) * scale).astype(half))
    up_halves = pair_halves(left_up_half, 0)
    right_kept, right_sent = right_halves
    right_got, *_ = lax.optimization_barrier((paired(right_sent, 2), *down_halves))
    right_cur = added(right_kept, right_got).astype(half)
    right_kept, right_sent = pair_halves(right_cur, 0, 1)
    right_got = paired(right_sent, 1)
    right_kept, right_sent = pair_halves(added(right_kept, right_got).astype(half), 0)
    right_got = paired(right_sent)
    down_got, up_got = paired(down_halves[1]), paired(up_halves[1])
    right_up_parts = collected(right_up_part)
    right_up_grad, left_up_grad, left_down_grad, right_down_grad = final_sums(
        right_up_parts, (up_halves[0], up_got), (down_halves[0], down_got), (right_kept, right_got)
    )
    tokens_grad = contract(grad_act_up, 0, weight_ru, 1).astype(half)
    return (
        layer_out,
        tokens_grad,
        right_up_grad[None],
        left_up_grad[None],
        left_down_grad[None],
        right_down_grad[None],
    )


def solution(mesh):
    placed = (
        P("dp", "hid"),
        P("dp", "hid"),
        P("hid", None, None),
        P("hid", None, None),
        P("hid", None, None),
        P("hid", None, None),
    )
    return jax.shard_map(
        body,
        mesh=mesh,
        in_specs=placed,
        out_specs=(
            P("dp", "hid"),
            P("dp", "hid"),
            P("hid", "dp", None),
            P("hid", "dp", None),
            P("hid", "dp", None),
            P("hid", "dp", None),
        ),
        check_vma=False,
    )
```

```python
import jax
import jax.numpy as jnp
from jax import lax
from jax.experimental.layout import Layout, with_layout_constraint
from jax.experimental import pallas as pl
from jax.experimental.pallas import tpu as pltpu
from jax.sharding import PartitionSpec as P


def contract(left_side, left_dim, right_side, right_dim):
    return lax.dot_general(
        left_side,
        right_side,
        (((left_dim,), (right_dim,)), ((), ())),
        preferred_element_type=jnp.float32,
    )


def row_major(value):
    return with_layout_constraint(value, Layout(tuple(range(value.ndim))))


def exchange(tile):
    return lax.all_to_all(tile, "hid", 0, 0, tiled=True)


def collected(part):
    rows = part.shape[0] // lax.axis_size("dp")
    return lax.all_to_all(part, "dp", 0, 0, tiled=True).reshape(-1, rows, part.shape[1])


def pair_halves(cur, axis, bit=0):
    side = jnp.bitwise_and(jnp.right_shift(lax.axis_index("dp"), bit), 1)
    return [
        lax.dynamic_index_in_dim(cur, place, axis, keepdims=False) for place in (side, 1 - side)
    ]


def paired(value, bit=0):
    return lax.ppermute(value, "dp", [(i, i ^ (1 << bit)) for i in range(lax.axis_size("dp"))])


def column_blocks(cur):
    column = jnp.right_shift(lax.axis_index("dp"), 1)
    own, ahead, back, far = (
        lax.dynamic_index_in_dim(
            cur, jnp.bitwise_and(column + step, cur.shape[0] - 1), 0, keepdims=False
        )
        for step in (0, 1, 3, 2)
    )
    return [own, ahead, back, far[0], far[1]]


def shifted(value, step):
    size = lax.axis_size("dp")
    return lax.ppermute(value, "dp", [(i, (i + 2 * step) % size) for i in range(size)])


def added(*terms):
    return sum((term.astype(jnp.float32) for term in terms[1:]), terms[0].astype(jnp.float32))


def first_leg(blocks, after=()):
    own, ahead, back, far_ahead, far_back = blocks
    got = (shifted(far_ahead, 1), shifted(far_back, -1))
    from_back, from_ahead = lax.optimization_barrier((*got, *after))[:2]
    half = own.dtype
    ahead = ahead.at[0].set(added(ahead[0], from_back).astype(half))
    back = back.at[1].set(added(back[1], from_ahead).astype(half))
    return [own, ahead, back]


def second_leg(blocks, after=()):
    own, ahead, back = blocks
    got = (shifted(ahead, 1), shifted(back, -1))
    got = lax.optimization_barrier((*got, *after))[:2]
    return added(own, *got)


def by_place(part):
    return part.reshape(lax.axis_size("dp") // 2, 2, -1, part.shape[1])


def final_kernel(parts, *refs):
    wide = jnp.float32
    *pairs, parts_out, first_out, second_out, third_out = refs
    total = parts[0].astype(wide)
    for place in range(1, parts.shape[0]):
        total = total + parts[place].astype(wide)
    parts_out[...] = total
    for place, out in enumerate((first_out, second_out, third_out)):
        kept, got = pairs[2 * place], pairs[2 * place + 1]
        out[...] = kept[...].astype(wide) + got[...].astype(wide)


def final_sums(parts, *pairs):
    shapes = [parts.shape[1:]] + [kept.shape for kept, _ in pairs]
    reads = sum(value.size for pair in pairs for value in pair) + parts.size
    writes = sum(shape[0] * shape[1] for shape in shapes)
    return pl.pallas_call(
        final_kernel,
        out_shape=[jax.ShapeDtypeStruct(shape, jnp.float32) for shape in shapes],
        compiler_params=pltpu.CompilerParams(vmem_limit_bytes=16 * 1024 * 1024),
        cost_estimate=pl.CostEstimate(
            flops=reads, bytes_accessed=2 * reads + 4 * writes, transcendentals=0
        ),
    )(parts, *(value for pair in pairs for value in pair))


def scaled_product(left_side, right_side, scale):
    def kernel(left, right, out):
        term = lax.dot_general(
            left[...],
            right[...],
            (((1,), (1,)), ((), ())),
            preferred_element_type=jnp.float32,
        )
        out[...] = (term * scale).astype(out.dtype)

    rows, depth = left_side.shape
    columns = right_side.shape[0]
    return pl.pallas_call(
        kernel,
        out_shape=jax.ShapeDtypeStruct((rows, columns), left_side.dtype),
        compiler_params=pltpu.CompilerParams(vmem_limit_bytes=16 * 1024 * 1024),
        cost_estimate=pl.CostEstimate(
            flops=2 * rows * columns * depth,
            bytes_accessed=2 * (rows * depth + columns * depth + rows * columns),
            transcendentals=0,
        ),
    )(left_side, right_side)


def body(tokens, cotangent, right_up, left_up, left_down, right_down):
    weight_ru = right_up[0]
    weight_lu = left_up[0]
    weight_ld = left_down[0]
    weight_rd = right_down[0]
    half = jnp.bfloat16
    scale = (tokens.shape[0] * lax.axis_size("dp")) ** (-0.5)
    act_up = contract(weight_ru, 0, tokens, 1).astype(half)
    mixed_up = exchange(act_up)
    grad_mixed_down = row_major(contract(weight_rd, 1, cotangent, 1).astype(half))
    grad_mixed_down, mixed_up = lax.optimization_barrier((grad_mixed_down, mixed_up))
    received = exchange(grad_mixed_down)
    pre = contract(weight_lu, 0, mixed_up, 0)
    sigma = jax.nn.sigmoid(pre)
    hidden = (pre * sigma).astype(half)
    act_down = contract(weight_ld, 0, hidden, 0).astype(half)
    act_down = row_major(act_down)
    slope = sigma * (1.0 + pre * (1.0 - sigma))
    tokens_turned = row_major(tokens.T)
    grad_act_down, hidden, slope, tokens_turned, _ = lax.optimization_barrier(
        (received, hidden, slope, tokens_turned, act_down)
    )
    mixed_down = exchange(act_down)
    left_down_part = (contract(hidden, 1, grad_act_down, 1) * scale).astype(half)
    grad_act_down, *down_blocks = lax.optimization_barrier(
        (grad_act_down, *column_blocks(by_place(left_down_part)))
    )
    down_blocks = first_leg(down_blocks)
    grad_hidden = contract(weight_ld, 1, grad_act_down, 0)
    grad_pre = (grad_hidden * slope).astype(half)
    left_up_part = (contract(mixed_up, 1, grad_pre, 1) * scale).astype(half)
    up_blocks = column_blocks(by_place(left_up_part))
    grad_mixed_up = row_major(contract(weight_lu, 1, grad_pre, 0).astype(half))
    grad_mixed_up, mixed_down, *_ = lax.optimization_barrier(
        (grad_mixed_up, mixed_down, *down_blocks, *up_blocks)
    )
    grad_act_up = exchange(grad_mixed_up)
    up_blocks = first_leg(up_blocks, (mixed_down,))
    later, *up_blocks = lax.optimization_barrier((mixed_down, *up_blocks))
    left_down_half = second_leg(down_blocks, (mixed_down,)).astype(half)
    down_halves = pair_halves(left_down_half, 0)
    right_down_part = row_major((contract(later, 1, cotangent, 0) * scale).astype(half))
    right_cur = right_down_part.reshape(2, 2, 2, -1, right_down_part.shape[1])
    right_halves = pair_halves(right_cur, 0, 2)
    layer_out = contract(mixed_down, 0, weight_rd, 0).astype(half)
    left_up_half = second_leg(up_blocks, down_halves).astype(half)
    right_up_part = scaled_product(tokens_turned, grad_act_up, scale)
    up_halves = pair_halves(left_up_half, 0)
    right_kept, right_sent = right_halves
    right_got, *_ = lax.optimization_barrier((paired(right_sent, 2), *down_halves))
    right_cur = added(right_kept, right_got).astype(half)
    right_kept, right_sent = pair_halves(right_cur, 0, 1)
    right_got = paired(right_sent, 1)
    right_kept, right_sent = pair_halves(added(right_kept, right_got).astype(half), 0)
    right_got = paired(right_sent)
    down_got, up_got = paired(down_halves[1]), paired(up_halves[1])
    right_up_parts = collected(right_up_part)
    right_up_grad, left_up_grad, left_down_grad, right_down_grad = final_sums(
        right_up_parts, (up_halves[0], up_got), (down_halves[0], down_got), (right_kept, right_got)
    )
    tokens_grad = contract(grad_act_up, 0, weight_ru, 1).astype(half)
    return (
        layer_out,
        tokens_grad,
        right_up_grad[None],
        left_up_grad[None],
        left_down_grad[None],
        right_down_grad[None],
    )


def solution(mesh):
    placed = (
        P("dp", "hid"),
        P("dp", "hid"),
        P("hid", None, None),
        P("hid", None, None),
        P("hid", None, None),
        P("hid", None, None),
    )
    return jax.shard_map(
        body,
        mesh=mesh,
        in_specs=placed,
        out_specs=(
            P("dp", "hid"),
            P("dp", "hid"),
            P("hid", "dp", None),
            P("hid", "dp", None),
            P("hid", "dp", None),
            P("hid", "dp", None),
        ),
        check_vma=False,
    )
```
